32 devices in a mesh: row: 8 (over y, x, core), col: 4 (over z).
Axes of the slice: x: 2, y: 2, z: 4, core: 2. Of those that a mesh axis runs over, the one named last changes fastest.
Arguments:
- aligned_family_embedding: bfloat16 [256, 384, 256], P('row', 'col'), may hold values from -24 to 24
- aligned_slot_available: int32 [256, 384], P('row', 'col'), may hold values from 0 to 1, as said below
- chain_site_available: int32 [384], replicated, may hold values 0 or 1
- duo_embedding: float32 [384, 384, 128], P('row', 'col'), may hold values from -1.2 to 1.2
- averaging_layernorm_stretch: float32 [256], replicated, may hold values from 0.1 to 1.9
- lineup_layernorm_stretch: float32 [256], replicated, may hold values from 0.1 to 1.9
- duo_layernorm_stretch: float32 [128], replicated, may hold values from 0.1 to 1.9
- lefthand_linear_kernel: bfloat16 [256, 32], replicated, may hold values from -0.375 to 0.375
- righthand_linear_kernel: bfloat16 [256, 32], replicated, may hold values from -0.375 to 0.375
- kronecker_linear_kernel: bfloat16 [1024, 128], replicated, may hold values from -0.1875 to 0.1875
- duo_logit_kernel: bfloat16 [128, 8], replicated, may hold values from -0.75 to 0.75
- asker_lookup_sigmoid_kernel: bfloat16 [256, 1024], replicated, may hold values from -8 to 8
- closing_linear_kernel: bfloat16 [256, 256], replicated, may hold values from -0.375 to 0.375
Outputs:
- refreshed_family_embedding: bfloat16 [256, 384, 256], P('row', 'col')
- duo_after_averaging: float32 [384, 384, 128], P('row', 'col')
The draws below stay inside these ranges and needn't reach their ends.
Inputs may be any that keep to these rules, and one draw needn't show every extreme that they name: `aligned_slot_available`: 0 or 1; sequence 0 is present at every residue.
All inputs are finite; a program needn't handle non-finite values.
Results may differ from the reference program's by a relative error of at most 0.0052.
Values may be sent and summed in bfloat16 or wider, within the bound.
No kernel may reach another device: no remote copies, remote signals or barrier semaphores. Data moves between devices by JAX's collectives and lax.ppermute only.
A program may use at most 192 MiB of HBM per device.

```python
import math
import jax
import jax.numpy as jnp
from jax import lax

C_M = 256
C_Z = 128
C_OPM = 32
HEADS = 8
HEAD_DIM = 32
R = 384
S = 256
N_ROW = 8


latent_rank = 8


def draw_aligned_family_embedding(key, part):
    subkeys = jax.random.split(key, 6)
    consensus = jnp.clip(jax.random.normal(subkeys[0], (1, R, C_M), jnp.float32), -5.0, 5.0) * 0.4
    factors = jnp.clip(jax.random.normal(subkeys[4], (S, latent_rank), jnp.float32), -4.0, 4.0)
    loadings = jnp.clip(jax.random.normal(subkeys[5], (latent_rank, R * C_M), jnp.float32), -4.0, 4.0) / math.sqrt(latent_rank)
    shared = jnp.dot(factors, loadings).reshape(S, R, C_M) * 1.5
    noise_part = jnp.clip(jax.random.normal(subkeys[1], (S, R, C_M), jnp.float32), -5.0, 5.0)
    values = consensus + shared + noise_part
    return jnp.clip(values, -24.0, 24.0).astype(jnp.bfloat16)


def draw_aligned_slot_available(key, part):
    subkeys = jax.random.split(key, 2)
    row_ids = jnp.arange(S, dtype=jnp.int32)[:, None]
    limits = 3 + 9 * row_ids // S + jax.random.randint(subkeys[0], (S, 1), 0, 4, dtype=jnp.int32)
    sampled = jax.random.randint(subkeys[1], (S, R), 0, 16, dtype=jnp.int32)
    kept_ones = jnp.where(sampled < limits, 1, 0)
    return jnp.where(row_ids == 0, 1, kept_ones).astype(jnp.int32)


def draw_asker_lookup_sigmoid_kernel(key, part):
    inner_width = HEADS * HEAD_DIM
    subkeys = jax.random.split(key, 2)
    base_part = jnp.clip(jax.random.normal(subkeys[0], (C_M, inner_width), jnp.float32), -5.0, 5.0) / math.sqrt(C_M)
    rest_part = jnp.clip(jax.random.normal(subkeys[1], (C_M, 3 * inner_width), jnp.float32), -5.0, 5.0) / math.sqrt(C_M)
    values = jnp.concatenate([base_part, rest_part], axis=1)
    return values.astype(jnp.bfloat16)


def set_ends(entries, key, low, high):
    longest = entries.shape.index(max(entries.shape))
    spots = []
    for shift in (0, 1):
        where = [jax.random.randint(jax.random.fold_in(key, axis), (), 0, length) for axis, length in enumerate(entries.shape)]
        where[longest] = (where[longest] + shift) % entries.shape[longest]
        spots.append(tuple(where))
    return entries.at[spots[0]].set(low).at[spots[1]].set(high)


def shard_levels(rng, shape, pieces, smallest, top_value):
    loudness, own = 1.0, jax.random.fold_in(rng, 6)
    for position, shards_of in pieces:
        heights = jnp.exp(jax.random.uniform(jax.random.fold_in(own, position), (shards_of,), jnp.float32, smallest / len(pieces), top_value / len(pieces)))
        loudness = loudness * jnp.repeat(heights, shape[position] // shards_of).reshape([-1 if axis == position else 1 for axis in range(len(shape))])
    return loudness


def noise(own_key, dims, spread, bound, pieces=(), held_as=jnp.bfloat16):
    values = jax.random.normal(own_key, dims, jnp.float32) * spread
    if len(pieces) > 0:
        values = shard_levels(own_key, dims, pieces, -0.22, 0.18) * values
    return jnp.clip(values, min=-bound, max=bound).astype(held_as)


def setup_inputs(seed: int = 0) -> dict:
    key_of = jax.random.split(jax.random.key(seed), 14)
    return {
        "aligned_family_embedding": draw_aligned_family_embedding(jax.random.fold_in(key_of[13], 71), 0),
        "aligned_slot_available": draw_aligned_slot_available(jax.random.fold_in(key_of[13], 71), 0),
        "chain_site_available": set_ends((jax.random.randint(key_of[2], (R,), 0, 8) < 7).astype(jnp.int32), jax.random.fold_in(key_of[2], 1), 0, 1),
        "duo_embedding": noise(key_of[3], (R, R, C_Z), 0.15, 1.2, ((0, 8), (1, 4)), jnp.float32),
        "averaging_layernorm_stretch": jnp.clip(1.0 + 0.18 * jax.random.normal(key_of[4], (C_M,), jnp.float32), 0.1, 1.9),
        "lineup_layernorm_stretch": jnp.clip(1.0 + 0.18 * jax.random.normal(key_of[5], (C_M,), jnp.float32), 0.1, 1.9),
        "duo_layernorm_stretch": jnp.clip(1.0 + 0.18 * jax.random.normal(key_of[6], (C_Z,), jnp.float32), 0.1, 1.9),
        "lefthand_linear_kernel": noise(key_of[7], (C_M, C_OPM), C_M ** -0.5, 0.375),
        "righthand_linear_kernel": noise(key_of[8], (C_M, C_OPM), C_M ** -0.5, 0.375),
        "kronecker_linear_kernel": noise(key_of[9], (C_OPM * C_OPM, C_Z), (C_OPM * C_OPM) ** -0.5, 0.1875),
        "duo_logit_kernel": noise(key_of[10], (C_Z, HEADS), (C_Z // 2) ** -0.5, 0.75),
        "asker_lookup_sigmoid_kernel": draw_asker_lookup_sigmoid_kernel(jax.random.fold_in(key_of[13], 71), 0),
        "closing_linear_kernel": noise(key_of[12], (HEADS * HEAD_DIM, C_M), (HEADS * HEAD_DIM) ** -0.5, 0.375),
    }


EPSILON = 1e-05
CONTRACT_FIRST = (((0,), (0,)), ((), ()))

def standardize_features(values):
    average = lax.optimization_barrier(jnp.mean(values, axis=-1, keepdims=True))
    centred = values - average
    variance = lax.optimization_barrier(jnp.mean(centred * centred, axis=-1, keepdims=True))
    return centred * lax.rsqrt(variance + EPSILON)

def rounded(values):
    return lax.optimization_barrier(values.astype(jnp.bfloat16)).astype(jnp.float32)

def reference(aligned_family_embedding, aligned_slot_available, chain_site_available, duo_embedding, averaging_layernorm_stretch, lineup_layernorm_stretch, duo_layernorm_stretch, lefthand_linear_kernel, righthand_linear_kernel, kronecker_linear_kernel, duo_logit_kernel, asker_lookup_sigmoid_kernel, closing_linear_kernel):
    standardized_features = standardize_features(aligned_family_embedding.astype(jnp.float32))
    availability_real = aligned_slot_available.astype(jnp.float32)
    opm_input = rounded(standardized_features * averaging_layernorm_stretch)
    left_flat = (jnp.einsum('src,ca->sra', opm_input, lefthand_linear_kernel.astype(jnp.float32)) * availability_real[:, :, None]).astype(jnp.bfloat16).reshape(S, R * C_OPM)
    right_flat = (jnp.einsum('src,ca->sra', opm_input, righthand_linear_kernel.astype(jnp.float32)) * availability_real[:, :, None]).astype(jnp.bfloat16).reshape(S, R * C_OPM)
    row_block = R // N_ROW
    left_blocks = left_flat.reshape(S, N_ROW, row_block * C_OPM).transpose(1, 0, 2)
    mask_blocks = availability_real.reshape(S, N_ROW, row_block).transpose(1, 0, 2)
    mixing = kronecker_linear_kernel.astype(jnp.float32).reshape(C_OPM, C_OPM, C_Z)

    def pair_block(group_members):
        left_part, mask_part = group_members
        outer_sum = lax.dot_general(left_part, right_flat, CONTRACT_FIRST, preferred_element_type=jnp.float32)
        counts = lax.dot_general(mask_part, availability_real, CONTRACT_FIRST, preferred_element_type=jnp.float32)
        outer_round = rounded(outer_sum).reshape(row_block, C_OPM, R, C_OPM)
        update = jnp.einsum('iajb,abk->ijk', outer_round, mixing)
        return update / (counts + 0.001)[:, :, None]
    update = lax.map(pair_block, (left_blocks, mask_blocks)).reshape(R, R, C_Z)
    residue_float = chain_site_available.astype(jnp.float32)
    duo_after_averaging = duo_embedding + update * (residue_float[:, None] * residue_float[None, :])[:, :, None]
    pair_input = rounded(standardize_features(duo_after_averaging) * duo_layernorm_stretch)
    pair_bias = rounded(jnp.einsum('ijc,ch->hij', pair_input, duo_logit_kernel.astype(jnp.float32)))
    exponential_probabilities = (standardized_features * lineup_layernorm_stretch).astype(jnp.bfloat16)
    inner_width = HEADS * HEAD_DIM
    score_scale = HEAD_DIM ** (-0.5)
    output_as_float = closing_linear_kernel.astype(jnp.float32)

    def solitary_alignee(group_members):
        row_entry, row_present_mask, alignment_row = group_members
        projected = rounded(jnp.dot(row_entry, asker_lookup_sigmoid_kernel, preferred_element_type=jnp.float32))
        queries = projected[:, :inner_width].reshape(R, HEADS, HEAD_DIM)
        keys_all = projected[:, inner_width:2 * inner_width].reshape(R, HEADS, HEAD_DIM)
        values_all = projected[:, 2 * inner_width:3 * inner_width].reshape(R, HEADS, HEAD_DIM)
        gate_pre = projected[:, 3 * inner_width:]
        scores = jnp.einsum('qhd,khd->hqk', queries, keys_all) * score_scale + pair_bias + 1000000000.0 * (row_present_mask[None, None, :] - 1.0)
        highest = lax.optimization_barrier(jnp.max(scores, axis=-1, keepdims=True))
        exponent = jnp.exp(scores - highest)
        weights = rounded(exponent / lax.optimization_barrier(jnp.sum(exponent, axis=-1, keepdims=True)))
        mixed_rows = jnp.einsum('hqk,khd->qhd', weights, values_all).reshape(R, inner_width)
        gated_row_output = rounded(mixed_rows * jax.nn.sigmoid(gate_pre))
        return (alignment_row.astype(jnp.float32) + jnp.einsum('lg,gf->lf', gated_row_output, output_as_float)).astype(jnp.bfloat16)
    refreshed_family_embedding = lax.map(solitary_alignee, (exponential_probabilities, availability_real, aligned_family_embedding))
    return (refreshed_family_embedding, duo_after_averaging)
```

```python
import math

import jax
import jax.numpy as jnp
from jax import lax
from jax.experimental import pallas as pl
from jax.experimental.pallas import tpu as pltpu
from jax.sharding import PartitionSpec as P

EPSILON = 1e-05
LOG2E = math.log2(math.e)
LANES = 128
ROWS_BY_ROWS = (((1,), (1,)), ((), ()))
CONTRACT_FIRST = (((0,), (0,)), ((), ()))
VMEM = pltpu.CompilerParams(vmem_limit_bytes=56 * 2**20)
SMEM = pl.BlockSpec(memory_space=pltpu.SMEM)
f32 = jnp.float32
bf16 = jnp.bfloat16


def whole(array):
    return pl.BlockSpec(array.shape, lambda step, rank=array.ndim: (0,) * rank)


def standardize(values):
    average = jnp.mean(values, axis=-1, keepdims=True)
    centred = values - average
    variance = jnp.mean(centred * centred, axis=-1, keepdims=True)
    return centred * lax.rsqrt(variance + EPSILON)


def opm_inputs_kernel(half_ref, x_ref, mask_ref, gain_ref, wl_ref, wr_ref, left_ref, right_ref, scratch):
    seqs, residues, channels = x_ref.shape
    width = wr_ref.shape[0]
    per_group = LANES // width
    groups = residues // per_group
    halves, slabs = left_ref.shape[:2]
    half_groups = slabs - 1
    half_residues = residues // halves
    normed = standardize(x_ref[...].reshape(seqs * residues, channels).astype(f32)) * gain_ref[...]
    for piece in range(channels // LANES):
        scratch[piece] = normed[:, piece * LANES : (piece + 1) * LANES]
    narrow = normed.astype(bf16).reshape(seqs, residues, channels)
    mask = mask_ref[...].astype(f32)
    right = [
        lax.dot_general(wr_ref[...], narrow[s], ROWS_BY_ROWS, preferred_element_type=f32) * mask[s : s + 1, :]
        for s in range(seqs)
    ]
    right_ref[:width] = jnp.swapaxes(jnp.stack(right, 0), 0, 1).astype(bf16)
    right_ref[width] = mask.astype(bf16)
    total = None
    for q in range(per_group):
        rows = jnp.concatenate(
            [scratch[piece, pl.ds(q, seqs * groups, stride=per_group), :] for piece in range(channels // LANES)], 1
        ).astype(bf16)
        part = jnp.dot(rows, wl_ref[q], preferred_element_type=f32)
        total = part if total is None else total + part
    left = jnp.swapaxes(total.reshape(seqs, groups, LANES), 0, 1)
    row = lax.broadcasted_iota(jnp.int32, (residues, residues * width), 0) * width
    col = lax.broadcasted_iota(jnp.int32, (residues, residues * width), 1)
    spread = ((col >= row) & (col < row + width)).astype(f32).astype(bf16)
    mask_wide = jnp.dot(mask.astype(bf16), spread, preferred_element_type=f32)
    flip = half_ref[0]
    for g in range(groups):
        half = g // half_groups
        slot = half + flip - 2 * half * flip
        left_ref[slot, g % half_groups] = (left[g] * mask_wide[:, g * LANES : (g + 1) * LANES]).astype(bf16)
    for half in range(halves):
        slot = half + flip - 2 * half * flip
        part = mask[:, half * half_residues : (half + 1) * half_residues]
        left_ref[slot, half_groups] = jnp.concatenate(
            [part, jnp.zeros((seqs, LANES - half_residues), f32)], 1
        ).astype(bf16)


def opm_inputs(flip, x, mask, gain, wl, wr, half_residues, block=16):
    seqs, residues, channels = x.shape
    width = wl.shape[1]
    per_group = LANES // width
    halves = residues // half_residues
    slabs = half_residues // per_group + 1
    wide = jnp.stack([jnp.pad(wl, ((0, 0), (q * width, LANES - (q + 1) * width))) for q in range(per_group)])
    gain = gain.reshape(1, channels)
    return pl.pallas_call(
        opm_inputs_kernel,
        grid=(seqs // block,),
        in_specs=[
            SMEM,
            pl.BlockSpec((block, residues, channels), lambda s: (s, 0, 0)),
            pl.BlockSpec((block, residues), lambda s: (s, 0)),
            whole(gain),
            whole(wide),
            pl.BlockSpec((width, channels), lambda s: (0, 0)),
        ],
        out_specs=[
            pl.BlockSpec((halves, slabs, block, LANES), lambda s: (0, 0, s, 0)),
            pl.BlockSpec((width + 1, block, residues), lambda s: (0, s, 0)),
        ],
        out_shape=[
            jax.ShapeDtypeStruct((halves, slabs, seqs, LANES), bf16),
            jax.ShapeDtypeStruct((width + 1, seqs, residues), bf16),
        ],
        scratch_shapes=[pltpu.VMEM((channels // LANES, block * residues, LANES), f32)],
        compiler_params=VMEM,
        name="opm_inputs",
    )(flip, x, mask, gain, wide, wr.T)


def pair_tile(order, lefts, rights, duo, chain_rows, chain_cols, kernel, gain, logit, block=16):
    rows, residues, channels = duo.shape
    heads = logit.shape[1]
    width = rights[0].shape[0] - 1
    seqs = rights[0].shape[1]
    groups = lefts[0].shape[0] - 1
    parts = len(rights)

    def body(order_ref, *refs):
        left_refs, right_refs = refs[:parts], refs[parts : 2 * parts]
        duo_ref, ci_ref, cj_ref, w_ref, gain_ref, logit_ref, out_ref, bias_ref, rhs, lhs, scale = refs[2 * parts :]
        step = pl.program_id(0)

        @pl.when(step == 0)
        def _():
            counts = jnp.zeros((LANES, residues), f32)
            for n, ref in enumerate(right_refs):
                for b in range(width):
                    rhs[n * seqs : (n + 1) * seqs, b * LANES : b * LANES + residues] = ref[b]
                rhs[n * seqs : (n + 1) * seqs, width * LANES : width * LANES + residues] = ref[width]
            for n, ref in enumerate(left_refs):
                place = pl.ds(pl.multiple_of(order_ref[n] * seqs, seqs), seqs)
                for g in range(groups + 1):
                    lhs[place, g * LANES : (g + 1) * LANES] = ref[g]
            counts = lax.dot_general(
                lhs[:, groups * LANES :], rhs[:, width * LANES :], CONTRACT_FIRST, preferred_element_type=f32
            )[:rows, :residues]
            scale[:, :residues] = ci_ref[...] * cj_ref[...] / (counts + 0.001)

        span = block * width
        picked = lhs[:, pl.ds(pl.multiple_of(step * span, LANES), span)]
        outer = lax.dot_general(
            picked, rhs[:, : width * LANES], CONTRACT_FIRST, preferred_element_type=f32
        ).astype(bf16)
        row_scale = scale[pl.ds(pl.multiple_of(step * block, 8), block), :]
        biases = []
        for first in range(0, block, 2):
            both = [
                jnp.concatenate(
                    [outer[i * width : (i + 1) * width, b * LANES : (b + 1) * LANES] for b in range(width)], 0
                )
                for i in (first, first + 1)
            ]
            update = jnp.dot(w_ref[...], jnp.concatenate(both, 1), preferred_element_type=f32)
            for k, i in enumerate((first, first + 1)):
                mine = (update[:, k * LANES : (k + 1) * LANES] * row_scale[i : i + 1, :]).T[:residues]
                fresh = duo_ref[i] + mine
                out_ref[i] = fresh
                pair_input = (standardize(fresh) * gain_ref[...]).astype(bf16)
                biases.append(
                    lax.dot_general(logit_ref[...], pair_input, ROWS_BY_ROWS, preferred_element_type=f32)
                )
        bias_ref[...] = jnp.swapaxes(jnp.stack(biases, 0), 0, 1).astype(bf16)

    mixing = kernel.reshape(width, width, channels).transpose(2, 1, 0).reshape(channels, width * width)
    operands = [
        *lefts,
        *rights,
        duo,
        chain_rows.reshape(rows, 1),
        chain_cols.reshape(1, residues),
        mixing,
        gain.reshape(1, channels),
        logit.T,
    ]
    specs = [whole(array) for array in operands]
    specs[2 * parts] = pl.BlockSpec((block, residues, channels), lambda s: (s, 0, 0))
    return pl.pallas_call(
        body,
        grid=(rows // block,),
        in_specs=[SMEM, *specs],
        out_specs=[
            pl.BlockSpec((block, residues, channels), lambda s: (s, 0, 0)),
            pl.BlockSpec((heads, block, residues), lambda s: (0, s, 0)),
        ],
        out_shape=[
            jax.ShapeDtypeStruct((rows, residues, channels), f32),
            jax.ShapeDtypeStruct((heads, rows, residues), bf16),
        ],
        scratch_shapes=[
            pltpu.VMEM((parts * seqs, (width + 1) * LANES), bf16),
            pltpu.VMEM((parts * seqs, (groups + 1) * LANES), bf16),
            pltpu.VMEM((rows, LANES), f32),
        ],
        compiler_params=VMEM,
        name="pair_tile",
    )(order, *operands)


def project_kernel(*refs):
    parts = len(refs) - 5
    x_refs = refs[:parts]
    gain_ref, wk_ref, wt_ref, keys_ref, rest_ref = refs[parts:]
    x = jnp.concatenate([ref[0] for ref in x_refs], 0).astype(f32)
    narrow = (standardize(x) * gain_ref[...]).astype(bf16)
    keys_ref[0] = jnp.dot(narrow, wk_ref[...], preferred_element_type=f32).astype(bf16)
    rest_ref[0] = lax.dot_general(wt_ref[...], narrow, ROWS_BY_ROWS, preferred_element_type=f32).astype(bf16)


def project(pieces, gain, kernel):
    seqs, residues, channels = pieces[0].shape
    inner = kernel.shape[1] // 4
    total = residues * len(pieces)
    by_column = jnp.concatenate([kernel[:, :inner], kernel[:, 2 * inner :]], 1).T
    by_row = kernel[:, inner : 2 * inner]
    gain = gain.reshape(1, channels)
    return pl.pallas_call(
        project_kernel,
        grid=(seqs,),
        in_specs=[pl.BlockSpec((1, residues, channels), lambda s: (s, 0, 0))] * len(pieces)
        + [whole(gain), whole(by_row), whole(by_column)],
        out_specs=[
            pl.BlockSpec((1, total, inner), lambda s: (s, 0, 0)),
            pl.BlockSpec((1, 3 * inner, total), lambda s: (s, 0, 0)),
        ],
        out_shape=[
            jax.ShapeDtypeStruct((seqs, total, inner), bf16),
            jax.ShapeDtypeStruct((seqs, 3 * inner, total), bf16),
        ],
        compiler_params=VMEM,
        name="project",
    )(*pieces, gain, by_row, by_column)


def attend(slots, pieces, keys, rest, mask, biases, closing, first, count):
    seqs, residues, channels = pieces[0].shape
    parts = len(pieces)
    blocks = len(biases)
    heads, rows, total = biases[0].shape
    inner = keys.shape[2]
    depth = inner // heads
    head_group = LANES // depth
    scale = depth**-0.5 * LOG2E

    def body(slots_ref, *refs):
        x_refs, refs = refs[:parts], refs[parts:]
        keys_ref, rest_ref, mask_ref, refs = refs[0], refs[1], refs[2], refs[3:]
        bias_refs, refs = refs[:blocks], refs[blocks:]
        closing_ref, out_refs, (raw, bias_t, gated, sems) = refs[0], refs[1 : 1 + parts], refs[1 + parts :]

        @pl.when(pl.program_id(0) == 0)
        def _():
            copies = [
                pltpu.make_async_copy(ref, raw.at[slots_ref[n]], sems.at[n]) for n, ref in enumerate(bias_refs)
            ]
            for copy in copies:
                copy.start()
            for copy in copies:
                copy.wait()
            for h in range(heads):
                bias_t[h] = (raw[:, h].astype(f32) * LOG2E).reshape(total, total).T

        row_mask = (mask_ref[0].astype(f32) - 1.0) * (1e9 * LOG2E)
        tall_mask = jnp.broadcast_to(row_mask, (LANES, total)).T
        tall_mask = jnp.concatenate([tall_mask] * (total // LANES), 1)
        for h in range(heads):
            group, place = h // head_group, h % head_group
            key = keys_ref[0][:, group * LANES : (group + 1) * LANES]
            query = rest_ref[0, h * depth : (h + 1) * depth, :]
            zero = jnp.zeros_like(query)
            alone = jnp.concatenate([query if n == place else zero for n in range(head_group)], 0)
            value = rest_ref[0, inner + h * depth : inner + (h + 1) * depth, :]
            value = jnp.concatenate([value, jnp.ones((16, total), bf16)], 0)
            scores = jnp.dot(key, alone, preferred_element_type=f32) * scale + bias_t[h] + tall_mask
            highest = jnp.max(scores, axis=0, keepdims=True)
            weights = jnp.exp2(scores - highest).astype(bf16)
            mixed = jnp.dot(value, weights, preferred_element_type=f32)
            gate = rest_ref[0, 2 * inner + h * depth : 2 * inner + (h + 1) * depth, :].astype(f32)
            gated[h * depth : (h + 1) * depth, :] = (
                mixed[:depth] / mixed[depth : depth + 1] * jax.nn.sigmoid(gate)
            ).astype(bf16)
        change = lax.dot_general(gated[...], closing_ref[...], CONTRACT_FIRST, preferred_element_type=f32)
        for n in range(parts):
            out_refs[n][0] = (
                x_refs[n][0].astype(f32) + change[n * residues : (n + 1) * residues]
            ).astype(bf16)

    return pl.pallas_call(
        body,
        grid=(count,),
        in_specs=[SMEM]
        + [pl.BlockSpec((1, residues, channels), lambda s: (s + first, 0, 0))] * parts
        + [
            pl.BlockSpec((1, total, inner), lambda s: (s + first, 0, 0)),
            pl.BlockSpec((1, 3 * inner, total), lambda s: (s + first, 0, 0)),
            pl.BlockSpec((1, 1, total), lambda s: (s + first, 0, 0)),
        ]
        + [pl.BlockSpec(memory_space=pl.ANY)] * blocks
        + [whole(closing)],
        out_specs=[pl.BlockSpec((1, residues, channels), lambda s: (s, 0, 0))] * parts,
        out_shape=[jax.ShapeDtypeStruct((count, residues, channels), bf16)] * parts,
        scratch_shapes=[
            pltpu.VMEM((blocks, heads, rows, total), bf16),
            pltpu.VMEM((heads, total, total), f32),
            pltpu.VMEM((inner, total), bf16),
            pltpu.SemaphoreType.DMA((blocks,)),
        ],
        compiler_params=VMEM,
        name="attend",
    )(slots, *pieces, keys, rest, mask, *biases, closing)


def make_shards(mesh):
    n_row, n_col = mesh.shape["row"], mesh.shape["col"]
    halves = n_row // n_col

    def by_row(x, k):
        return lax.ppermute(x, "row", [(r, r ^ k) for r in range(n_row)])

    def by_col(x, k):
        return lax.ppermute(x, "col", [(c, c ^ k) for c in range(n_col)])

    def by_both(x, target):
        pairs = []
        for r in range(n_row):
            for c in range(n_col):
                to_row, to_col = target(r, c)
                pairs.append((r * n_col + c, to_row * n_col + to_col))
        return lax.ppermute(x, ("row", "col"), pairs)

    def gather_rows(x):
        pieces = {0: x}
        for k in range(halves, n_row, halves):
            pieces[k] = by_row(x, k)
        for k in range(0, n_row, halves):
            pieces[k + 1] = by_row(pieces[k], 1)
        return [pieces[k] for k in range(n_row)]

    def shards(
        msa,
        available,
        chain_site_available,
        duo_embedding,
        averaging_gain,
        lineup_gain,
        duo_gain,
        left_kernel,
        right_kernel,
        kronecker_kernel,
        logit_kernel,
        projection_kernel,
        closing_kernel,
    ):
        seqs, residues, channels = msa.shape
        rows = duo_embedding.shape[0]
        r, c = lax.axis_index("row"), lax.axis_index("col")
        share = seqs // n_col

        flip = (r % halves).astype(jnp.int32).reshape(1)
        left, right = opm_inputs(
            flip, msa, available, averaging_gain, left_kernel, right_kernel, rows
        )
        spread = [by_both(left, lambda a, b, u=u: (a, b ^ u ^ (a // halves))) for u in range(n_col)]
        rights = gather_rows(right)
        lefts = [
            by_both(spread[u][v], lambda a, b, u=u, v=v: (a ^ (halves * (b ^ u) + v), b))
            for u in range(n_col)
            for v in range(halves)
        ]
        order = jnp.stack([halves * (c ^ u) + v for u in range(n_col) for v in range(halves)]).astype(jnp.int32)

        mask = available.astype(bf16)
        held = lax.optimization_barrier((msa, *spread))[0]
        x_pieces, mask_pieces = [], []
        for k in range(n_col):
            place = (c ^ k) * share
            x_pieces.append(lax.dynamic_slice_in_dim(held, place, share, 0))
            mask_pieces.append(lax.dynamic_slice_in_dim(mask, place, share, 0))
            if k:
                x_pieces[k] = by_col(x_pieces[k], k)
                mask_pieces[k] = by_col(mask_pieces[k], k)
        rows_mask = jnp.concatenate(mask_pieces, 1)[:, None, :]

        chain = chain_site_available.astype(f32)
        duo_after_averaging, tile = pair_tile(
            order,
            lefts,
            rights,
            duo_embedding,
            lax.dynamic_slice_in_dim(chain, r * rows, rows),
            lax.dynamic_slice_in_dim(chain, c * residues, residues),
            kronecker_kernel,
            duo_gain,
            logit_kernel,
        )
        strip = jnp.concatenate([tile] + [by_col(tile, k) for k in range(1, n_col)], 2)
        biases = gather_rows(strip)
        slots = jnp.stack(
            [halves * (((r ^ w) // halves) ^ c) + (r ^ w) % halves for w in range(n_row)]
        ).astype(jnp.int32)

        keys, rest = project(x_pieces, lineup_gain, projection_kernel)
        chunk = max(share // CHUNKS, 1)
        refreshed = jnp.zeros_like(msa)
        for first in range(0, share, chunk):
            outs = attend(
                slots, x_pieces, keys, rest, rows_mask, biases, closing_kernel, first, chunk
            )
            for k, piece in enumerate(outs):
                if k:
                    piece = by_col(piece, k)
                refreshed = lax.dynamic_update_slice_in_dim(refreshed, piece, (c ^ k) * share + first, 0)
        return refreshed, duo_after_averaging

    return shards


CHUNKS = 4


def solution(mesh):
    split = P("row", "col", None)
    placed = (split, P("row", "col"), P(), split, P(), P(), P(), P(), P(), P(), P(), P(), P())
    return jax.shard_map(
        make_shards(mesh), mesh=mesh, in_specs=placed, out_specs=(split, split), check_vma=False
    )
```

```python
import math

import jax
import jax.numpy as jnp
from jax import lax
from jax.experimental import pallas as pl
from jax.experimental.pallas import tpu as pltpu
from jax.sharding import PartitionSpec as P

EPSILON = 1e-05
LOG2E = math.log2(math.e)
LANES = 128
ROWS_BY_ROWS = (((1,), (1,)), ((), ()))
CONTRACT_FIRST = (((0,), (0,)), ((), ()))
VMEM = pltpu.CompilerParams(vmem_limit_bytes=56 * 2**20)
SMEM = pl.BlockSpec(memory_space=pltpu.SMEM)
f32 = jnp.float32
bf16 = jnp.bfloat16


def whole(array):
    return pl.BlockSpec(array.shape, lambda step, rank=array.ndim: (0,) * rank)


def standardize(values):
    average = jnp.mean(values, axis=-1, keepdims=True)
    centred = values - average
    variance = jnp.mean(centred * centred, axis=-1, keepdims=True)
    return centred * lax.rsqrt(variance + EPSILON)


def opm_inputs_kernel(x_ref, mask_ref, gain_ref, wl_ref, wr_ref, left_ref, right_ref, scratch):
    seqs, residues, channels = x_ref.shape
    width = wr_ref.shape[0]
    per_group = LANES // width
    left_weight = wl_ref[...].astype(f32).T
    groups = residues // per_group
    halves, slabs = left_ref.shape[:2]
    half_groups = slabs - 1
    half_residues = residues // halves
    normed = standardize(x_ref[...].reshape(seqs * residues, channels).astype(f32)) * gain_ref[...]
    for piece in range(channels // LANES):
        scratch[piece] = normed[:, piece * LANES : (piece + 1) * LANES]
    narrow = normed.astype(bf16).reshape(seqs, residues, channels)
    mask = mask_ref[...].astype(f32)
    right = [
        lax.dot_general(wr_ref[...], narrow[s], ROWS_BY_ROWS, preferred_element_type=f32) * mask[s : s + 1, :]
        for s in range(seqs)
    ]
    right_ref[:width] = jnp.swapaxes(jnp.stack(right, 0), 0, 1).astype(bf16)
    right_ref[width] = mask.astype(bf16)
    total = None
    for q in range(per_group):
        rows = jnp.concatenate(
            [scratch[piece, pl.ds(q, seqs * groups, stride=per_group), :] for piece in range(channels // LANES)], 1
        ).astype(bf16)
        sides = [jnp.zeros((channels, q * width), f32), jnp.zeros((channels, LANES - (q + 1) * width), f32)]
        placed = jnp.concatenate([a for a in (sides[0], left_weight, sides[1]) if a.shape[1]], 1).astype(bf16)
        part = jnp.dot(rows, placed, preferred_element_type=f32)
        total = part if total is None else total + part
    left = jnp.swapaxes(total.reshape(seqs, groups, LANES), 0, 1)
    row = lax.broadcasted_iota(jnp.int32, (residues, residues * width), 0) * width
    col = lax.broadcasted_iota(jnp.int32, (residues, residues * width), 1)
    spread = ((col >= row) & (col < row + width)).astype(f32).astype(bf16)
    mask_wide = jnp.dot(mask.astype(bf16), spread, preferred_element_type=f32)
    for g in range(groups):
        left_ref[g // half_groups, g % half_groups] = (left[g] * mask_wide[:, g * LANES : (g + 1) * LANES]).astype(bf16)
    for half in range(halves):
        part = mask[:, half * half_residues : (half + 1) * half_residues]
        left_ref[half, half_groups] = jnp.concatenate(
            [part, jnp.zeros((seqs, LANES - half_residues), f32)], 1
        ).astype(bf16)


def opm_inputs(x, mask, gain, wl, wr, half_residues, block=16):
    seqs, residues, channels = x.shape
    width = wl.shape[1]
    per_group = LANES // width
    halves = residues // half_residues
    slabs = half_residues // per_group + 1
    gain = gain.reshape(1, channels)
    return pl.pallas_call(
        opm_inputs_kernel,
        grid=(seqs // block,),
        in_specs=[
            pl.BlockSpec((block, residues, channels), lambda s: (s, 0, 0)),
            pl.BlockSpec((block, residues), lambda s: (s, 0)),
            whole(gain),
            whole(wl.T),
            whole(wr.T),
        ],
        out_specs=[
            pl.BlockSpec((halves, slabs, block, LANES), lambda s: (0, 0, s, 0)),
            pl.BlockSpec((width + 1, block, residues), lambda s: (0, s, 0)),
        ],
        out_shape=[
            jax.ShapeDtypeStruct((halves, slabs, seqs, LANES), bf16),
            jax.ShapeDtypeStruct((width + 1, seqs, residues), bf16),
        ],
        scratch_shapes=[pltpu.VMEM((channels // LANES, block * residues, LANES), f32)],
        compiler_params=VMEM,
        name="opm_inputs",
    )(x, mask, gain, wl.T, wr.T)


def pair_tile(mine, left, right, duo, chain, kernel, gain, logit, block=16):
    rows, residues, channels = duo.shape
    heads = logit.shape[1]
    parts, slabs, seqs = left.shape[:3]
    groups = slabs - 1
    width = right.shape[1] - 1

    def body(mine_ref, left_ref, right_ref, *refs):
        duo_ref, chain_ref, kernel_ref, gain_ref, logit_ref, out_ref, bias_ref, rhs, lhs, scale, w_ref = refs
        step = pl.program_id(0)

        @pl.when(step == 0)
        def _():
            for n in range(parts):
                for b in range(width + 1):
                    rhs[n * seqs : (n + 1) * seqs, b * LANES : b * LANES + residues] = right_ref[n, b]
                for g in range(slabs):
                    lhs[n * seqs : (n + 1) * seqs, g * LANES : (g + 1) * LANES] = left_ref[n, g]
            counts = lax.dot_general(
                lhs[:, groups * LANES :], rhs[:, width * LANES :], CONTRACT_FIRST, preferred_element_type=f32
            )[:rows, :residues]
            flags = chain_ref[...].astype(f32)
            both_flags = []
            for size, at in ((rows, mine_ref[0] * rows), (residues, mine_ref[1] * residues)):
                place = lax.broadcasted_iota(jnp.int32, (chain.shape[1], size), 0)
                pick = place == lax.broadcasted_iota(jnp.int32, (chain.shape[1], size), 1) + at
                both_flags.append(jnp.dot(flags, pick.astype(f32), preferred_element_type=f32))
            present = lax.dot_general(*both_flags, CONTRACT_FIRST, preferred_element_type=f32)
            scale[:, :residues] = present / (counts + 0.001)
            mixing = jnp.swapaxes(kernel_ref[...].astype(f32).reshape(width, width, channels), 0, 1)
            w_ref[...] = mixing.reshape(width * width, channels).T.astype(bf16)

        span = block * width
        picked = lhs[:, pl.ds(pl.multiple_of(step * span, LANES), span)]
        outer = lax.dot_general(
            picked, rhs[:, : width * LANES], CONTRACT_FIRST, preferred_element_type=f32
        ).astype(bf16)
        row_scale = scale[pl.ds(pl.multiple_of(step * block, 8), block), :]
        biases = []
        for first in range(0, block, 2):
            both = [
                jnp.concatenate(
                    [outer[i * width : (i + 1) * width, b * LANES : (b + 1) * LANES] for b in range(width)], 0
                )
                for i in (first, first + 1)
            ]
            update = jnp.dot(w_ref[...], jnp.concatenate(both, 1), preferred_element_type=f32)
            for k, i in enumerate((first, first + 1)):
                fresh = duo_ref[i] + (update[:, k * LANES : (k + 1) * LANES] * row_scale[i : i + 1, :]).T[:residues]
                out_ref[i] = fresh
                pair_input = (standardize(fresh) * gain_ref[...]).astype(bf16)
                biases.append(
                    lax.dot_general(logit_ref[...], pair_input, ROWS_BY_ROWS, preferred_element_type=f32)
                )
        bias_ref[...] = jnp.swapaxes(jnp.stack(biases, 0), 0, 1).astype(bf16)

    operands = [
        left,
        right,
        duo,
        chain,
        kernel,
        gain.reshape(1, channels),
        logit.T,
    ]
    specs = [whole(array) for array in operands]
    specs[2] = pl.BlockSpec((block, residues, channels), lambda s: (s, 0, 0))
    return pl.pallas_call(
        body,
        grid=(rows // block,),
        in_specs=[SMEM, *specs],
        out_specs=[
            pl.BlockSpec((block, residues, channels), lambda s: (s, 0, 0)),
            pl.BlockSpec((heads, block, residues), lambda s: (0, s, 0)),
        ],
        out_shape=[
            jax.ShapeDtypeStruct((rows, residues, channels), f32),
            jax.ShapeDtypeStruct((heads, rows, residues), bf16),
        ],
        scratch_shapes=[
            pltpu.VMEM((parts * seqs, (width + 1) * LANES), bf16),
            pltpu.VMEM((parts * seqs, slabs * LANES), bf16),
            pltpu.VMEM((rows, LANES), f32),
            pltpu.VMEM((channels, width * width), bf16),
        ],
        compiler_params=VMEM,
        name="pair_tile",
    )(mine, *operands)


def attend(mine, pieces, gain, kernel, mask, low, high, closing, first, count):
    cols = len(pieces)
    residues, channels = pieces[0].shape[1:]
    arrays = [array for array, offsets in (*low, *high)]
    lists = [offsets for array, offsets in (*low, *high)]
    per_half, side, total = arrays[0].shape[1:]
    heads = 2 * per_half
    inner = closing.shape[0]
    depth = inner // heads
    gain = gain.reshape(1, channels)
    group = LANES // depth
    scale = depth**-0.5 * LOG2E

    def body(mine_ref, gain_ref, kernel_ref, mask_ref, closing_ref, *refs):
        x_refs, refs = refs[:cols], refs[cols:]
        bias_refs, out_refs = refs[: len(arrays)], refs[len(arrays) : -2]
        bias, turned = refs[-2:]

        @pl.when(pl.program_id(0) == 0)
        def _():
            for n, (ref, offsets) in enumerate(zip(bias_refs, lists)):
                start = n // len(low) * per_half
                for e, offset in enumerate(offsets):
                    place = pl.ds(pl.multiple_of((offset ^ mine_ref[2]) * side, 8), side)
                    for h in range(per_half):
                        bias[start + h, place, :] = ref[e, h].astype(f32) * LOG2E
            turned[...] = kernel_ref[:, inner : 2 * inner].T

        row_mask = (mask_ref[0].astype(f32) - 1.0) * (1e9 * LOG2E)
        head_of = lax.broadcasted_iota(jnp.int32, (total, LANES), 1) // depth
        zero = jnp.zeros((depth, total), bf16)
        x = jnp.concatenate([ref[0] for ref in x_refs], 0).astype(f32)
        narrow = (standardize(x) * gain_ref[...]).astype(bf16)
        keys = lax.dot_general(turned[...], narrow, ROWS_BY_ROWS, preferred_element_type=f32).astype(bf16)
        queries, all_values, gates = [
            jnp.dot(narrow, kernel_ref[:, n * inner : (n + 1) * inner], preferred_element_type=f32).astype(bf16)
            for n in (0, 2, 3)
        ]
        gated = []
        for first_lane in range(0, inner, LANES):
            span = slice(first_lane, first_lane + LANES)
            key = keys[span, :]
            value = all_values[:, span]
            alone, values = [], []
            for h in range(group):
                mine_rows = key[h * depth : (h + 1) * depth]
                alone.append(jnp.concatenate([mine_rows if n == h else zero for n in range(group)], 0))
                here = head_of == h
                values.append(
                    jnp.concatenate(
                        [jnp.where(here, value, jnp.zeros_like(value)), here.astype(f32).astype(bf16)], 1
                    )
                )
            scores = jnp.dot(queries[:, span], jnp.concatenate(alone, 1), preferred_element_type=f32)
            weights = []
            for h in range(group):
                own = scores[:, h * total : (h + 1) * total] * scale
                own = own + bias[first_lane // depth + h] + row_mask
                highest = jnp.max(own, axis=1, keepdims=True)
                weights.append(jnp.exp2(own - highest).astype(bf16))
            mixed = jnp.dot(
                jnp.concatenate(weights, 1), jnp.concatenate(values, 0), preferred_element_type=f32
            )
            gate = gates[:, span].astype(f32)
            gated.append((mixed[:, :LANES] / mixed[:, LANES:] * jax.nn.sigmoid(gate)).astype(bf16))
        change = jnp.dot(jnp.concatenate(gated, 1), closing_ref[...], preferred_element_type=f32)
        for k in range(cols):
            own = x[k * residues : (k + 1) * residues] + change[k * residues : (k + 1) * residues]
            out_refs[k][0] = own.astype(bf16)

    return pl.pallas_call(
        body,
        grid=(count,),
        in_specs=[
            SMEM,
            whole(gain),
            whole(kernel),
            pl.BlockSpec((1, 1, total), lambda s: (s + first, 0, 0)),
            whole(closing),
        ]
        + [pl.BlockSpec((1, residues, channels), lambda s: (s + first, 0, 0))] * cols
        + [whole(array) for array in arrays],
        out_specs=[pl.BlockSpec((1, residues, channels), lambda s: (s, 0, 0))] * cols,
        out_shape=[jax.ShapeDtypeStruct((count, residues, channels), bf16)] * cols,
        scratch_shapes=[pltpu.VMEM((heads, total, total), f32), pltpu.VMEM((inner, channels), bf16)],
        compiler_params=VMEM,
        name="attend",
    )(mine, gain, kernel, mask, closing, *pieces, *arrays)


def make_shards(mesh):
    n_row, n_col = mesh.shape["row"], mesh.shape["col"]
    halves = n_row // n_col

    def by_row(x, k):
        return lax.ppermute(x, "row", [(r, r ^ k) for r in range(n_row)])

    def by_col(x, k):
        return lax.ppermute(x, "col", [(c, c ^ k) for c in range(n_col)])

    def gather_rows(first, second):
        bits = []
        k = 2
        while k < n_row:
            bits.append(k)
            k *= 2
        held = [(first[None], [0]), (second[None], [0])]
        for step in range(len(bits)):
            got = []
            for part, k in ((0, bits[step]), (1, bits[-1 - step])):
                array, offsets = held[part]
                got.append(
                    (jnp.concatenate([array, by_row(array, k)], 0), offsets + [o ^ k for o in offsets])
                )
            held = got
        return [
            [(array, offsets), (by_row(array, 1), [o ^ 1 for o in offsets])] for array, offsets in held
        ]

    def shards(
        msa,
        available,
        chain_site_available,
        duo_embedding,
        averaging_gain,
        lineup_gain,
        duo_gain,
        left_kernel,
        right_kernel,
        kronecker_kernel,
        logit_kernel,
        projection_kernel,
        closing_kernel,
    ):
        seqs, residues, channels = msa.shape
        rows = duo_embedding.shape[0]
        r, c = lax.axis_index("row"), lax.axis_index("col")
        share = seqs // n_col
        mine = jnp.stack([r, c, r ^ (halves * c)]).astype(jnp.int32)

        left, right = opm_inputs(msa, available, averaging_gain, left_kernel, right_kernel, rows)
        rights = lax.all_gather(right, "row", axis=0)
        spread = lax.all_gather(left, "col", axis=0, tiled=True)
        left_rows = lax.all_to_all(spread, "row", 0, 0, tiled=True)

        msa_late, spread_late = lax.optimization_barrier((msa, spread))
        x = [lax.dynamic_slice_in_dim(msa_late, (c ^ k) * share, share, 0) for k in range(n_col)]
        x = [by_col(piece, k) if k else piece for k, piece in enumerate(x)]
        mask = lax.dynamic_slice_in_dim(spread_late[:, -1, :, :rows], c * share, share, 1)
        mask = mask.reshape(n_col, halves, share, rows)
        mask = jnp.stack([lax.dynamic_index_in_dim(mask, c ^ k, 0, keepdims=False) for k in range(n_col)])
        rows_mask = mask.transpose(2, 0, 1, 3).reshape(share, 1, residues * n_col)

        duo_after_averaging, tile = pair_tile(
            mine,
            left_rows,
            rights,
            duo_embedding,
            chain_site_available.reshape(1, -1),
            kronecker_kernel,
            duo_gain,
            logit_kernel,
        )
        tile, x[1:] = lax.optimization_barrier((tile, x[1:]))
        tiles = [tile] + [by_col(tile, k) for k in range(1, n_col)]
        cut = tile.shape[0] // 2
        low, high = gather_rows(
            jnp.concatenate([t[:cut] for t in tiles], 2), jnp.concatenate([t[cut:] for t in tiles], 2)
        )
        sent = []
        first = 0
        for count in chunks(share):
            held = rows_mask
            if len(sent) > 1:
                held, sent[-2] = lax.optimization_barrier((rows_mask, sent[-2]))
            outs = attend(
                mine, x, lineup_gain, projection_kernel, held, low, high, closing_kernel, first, count
            )
            sent.append([by_col(piece, k) if k else piece for k, piece in enumerate(outs)])
            first += count
        refreshed = jnp.zeros_like(msa)
        first = 0
        for count, parts in zip(chunks(share), sent):
            for k, piece in enumerate(parts):
                refreshed = lax.dynamic_update_slice_in_dim(refreshed, piece, (c ^ k) * share + first, 0)
            first += count
        return refreshed, duo_after_averaging

    return shards


def chunks(share):
    most = max(-(-3 * share // 8), 1)
    counts = []
    while sum(counts) < share:
        counts.append(min(most, share - sum(counts)))
    return counts


def solution(mesh):
    split = P("row", "col", None)
    placed = (split, P("row", "col"), P(), split, P(), P(), P(), P(), P(), P(), P(), P(), P())
    return jax.shard_map(
        make_shards(mesh), mesh=mesh, in_specs=placed, out_specs=(split, split), check_vma=False
    )
```

```python
import math

import jax
import jax.numpy as jnp
from jax import lax
from jax.experimental import pallas as pl
from jax.experimental.pallas import tpu as pltpu
from jax.sharding import PartitionSpec as P

EPSILON = 1e-05
LOG2E = math.log2(math.e)
LANES = 128
ROWS_BY_ROWS = (((1,), (1,)), ((), ()))
CONTRACT_FIRST = (((0,), (0,)), ((), ()))
VMEM = pltpu.CompilerParams(vmem_limit_bytes=56 * 2**20)
SMEM = pl.BlockSpec(memory_space=pltpu.SMEM)
f32 = jnp.float32
bf16 = jnp.bfloat16


def whole(array):
    return pl.BlockSpec(array.shape, lambda step, rank=array.ndim: (0,) * rank)


def standardize(values):
    average = jnp.mean(values, axis=-1, keepdims=True)
    centred = values - average
    variance = jnp.mean(centred * centred, axis=-1, keepdims=True)
    return centred * lax.rsqrt(variance + EPSILON)


def opm_inputs_kernel(x_ref, mask_ref, gain_ref, wl_ref, wr_ref, left_ref, right_ref, scratch):
    seqs, residues, channels = x_ref.shape
    width = wr_ref.shape[0]
    per_group = LANES // width
    left_weight = wl_ref[...].astype(f32).T
    groups = residues // per_group
    halves, slabs = left_ref.shape[:2]
    half_groups = slabs - 1
    half_residues = residues // halves
    normed = standardize(x_ref[...].reshape(seqs * residues, channels).astype(f32)) * gain_ref[...]
    for piece in range(channels // LANES):
        scratch[piece] = normed[:, piece * LANES : (piece + 1) * LANES]
    narrow = normed.astype(bf16).reshape(seqs, residues, channels)
    mask = mask_ref[...].astype(f32)
    right = [
        lax.dot_general(wr_ref[...], narrow[s], ROWS_BY_ROWS, preferred_element_type=f32) * mask[s : s + 1, :]
        for s in range(seqs)
    ]
    right_ref[:width] = jnp.swapaxes(jnp.stack(right, 0), 0, 1).astype(bf16)
    right_ref[width] = mask.astype(bf16)
    total = None
    for q in range(per_group):
        rows = jnp.concatenate(
            [scratch[piece, pl.ds(q, seqs * groups, stride=per_group), :] for piece in range(channels // LANES)], 1
        ).astype(bf16)
        sides = [jnp.zeros((channels, q * width), f32), jnp.zeros((channels, LANES - (q + 1) * width), f32)]
        placed = jnp.concatenate([a for a in (sides[0], left_weight, sides[1]) if a.shape[1]], 1).astype(bf16)
        part = jnp.dot(rows, placed, preferred_element_type=f32)
        total = part if total is None else total + part
    left = jnp.swapaxes(total.reshape(seqs, groups, LANES), 0, 1)
    row = lax.broadcasted_iota(jnp.int32, (residues, residues * width), 0) * width
    col = lax.broadcasted_iota(jnp.int32, (residues, residues * width), 1)
    spread = ((col >= row) & (col < row + width)).astype(f32).astype(bf16)
    mask_wide = jnp.dot(mask.astype(bf16), spread, preferred_element_type=f32)
    for g in range(groups):
        left_ref[g // half_groups, g % half_groups] = (left[g] * mask_wide[:, g * LANES : (g + 1) * LANES]).astype(bf16)
    for half in range(halves):
        part = mask[:, half * half_residues : (half + 1) * half_residues]
        left_ref[half, half_groups] = jnp.concatenate(
            [part, jnp.zeros((seqs, LANES - half_residues), f32)], 1
        ).astype(bf16)


def opm_inputs(x, mask, gain, wl, wr, half_residues, block=16):
    seqs, residues, channels = x.shape
    width = wl.shape[1]
    per_group = LANES // width
    halves = residues // half_residues
    slabs = half_residues // per_group + 1
    gain = gain.reshape(1, channels)
    return pl.pallas_call(
        opm_inputs_kernel,
        grid=(seqs // block,),
        in_specs=[
            pl.BlockSpec((block, residues, channels), lambda s: (s, 0, 0)),
            pl.BlockSpec((block, residues), lambda s: (s, 0)),
            whole(gain),
            whole(wl.T),
            whole(wr.T),
        ],
        out_specs=[
            pl.BlockSpec((halves, slabs, block, LANES), lambda s: (0, 0, s, 0)),
            pl.BlockSpec((width + 1, block, residues), lambda s: (0, s, 0)),
        ],
        out_shape=[
            jax.ShapeDtypeStruct((halves, slabs, seqs, LANES), bf16),
            jax.ShapeDtypeStruct((width + 1, seqs, residues), bf16),
        ],
        scratch_shapes=[pltpu.VMEM((channels // LANES, block * residues, LANES), f32)],
        compiler_params=VMEM,
        name="opm_inputs",
    )(x, mask, gain, wl.T, wr.T)


def pair_tile(mine, left, right, duo, chain, kernel, gain, logit, block=16):
    rows, residues, channels = duo.shape
    heads = logit.shape[1]
    parts, slabs, seqs = left.shape[:3]
    groups = slabs - 1
    width = right.shape[1] - 1

    def body(mine_ref, left_ref, right_ref, *refs):
        duo_ref, chain_ref, kernel_ref, gain_ref, logit_ref, out_ref, bias_ref, rhs, lhs, scale, w_ref = refs
        step = pl.program_id(0)

        @pl.when(step == 0)
        def _():
            for n in range(parts):
                for b in range(width + 1):
                    rhs[n * seqs : (n + 1) * seqs, b * LANES : b * LANES + residues] = right_ref[n, b]
                for g in range(slabs):
                    lhs[n * seqs : (n + 1) * seqs, g * LANES : (g + 1) * LANES] = left_ref[n, g]
            counts = lax.dot_general(
                lhs[:, groups * LANES :], rhs[:, width * LANES :], CONTRACT_FIRST, preferred_element_type=f32
            )[:rows, :residues]
            flags = chain_ref[...].astype(f32)
            both_flags = []
            for size, at in ((rows, mine_ref[0] * rows), (residues, mine_ref[1] * residues)):
                place = lax.broadcasted_iota(jnp.int32, (chain.shape[1], size), 0)
                pick = place == lax.broadcasted_iota(jnp.int32, (chain.shape[1], size), 1) + at
                both_flags.append(jnp.dot(flags, pick.astype(f32), preferred_element_type=f32))
            present = lax.dot_general(*both_flags, CONTRACT_FIRST, preferred_element_type=f32)
            scale[:, :residues] = present / (counts + 0.001)
            mixing = jnp.swapaxes(kernel_ref[...].astype(f32).reshape(width, width, channels), 0, 1)
            w_ref[...] = mixing.reshape(width * width, channels).T.astype(bf16)

        span = block * width
        picked = lhs[:, pl.ds(pl.multiple_of(step * span, LANES), span)]
        outer = lax.dot_general(
            picked, rhs[:, : width * LANES], CONTRACT_FIRST, preferred_element_type=f32
        ).astype(bf16)
        row_scale = scale[pl.ds(pl.multiple_of(step * block, 8), block), :]
        biases = []
        every = [
            jnp.concatenate(
                [outer[i * width : (i + 1) * width, b * LANES : (b + 1) * LANES] for b in range(width)], 0
            )
            for i in range(block)
        ]
        update = jnp.dot(w_ref[...], jnp.concatenate(every, 1), preferred_element_type=f32)
        fresh = []
        for i in range(block):
            mine = (update[:, i * LANES : (i + 1) * LANES] * row_scale[i : i + 1, :]).T[:residues]
            fresh.append(duo_ref[i] + mine)
            out_ref[i] = fresh[-1]
        pair_input = (standardize(jnp.concatenate(fresh, 0)) * gain_ref[...]).astype(bf16)
        for i in range(block):
            own = pair_input[i * residues : (i + 1) * residues]
            biases.append(lax.dot_general(logit_ref[...], own, ROWS_BY_ROWS, preferred_element_type=f32))
        bias_ref[...] = jnp.swapaxes(jnp.stack(biases, 0), 0, 1).astype(bf16)

    operands = [
        left,
        right,
        duo,
        chain,
        kernel,
        gain.reshape(1, channels),
        logit.T,
    ]
    specs = [whole(array) for array in operands]
    specs[2] = pl.BlockSpec((block, residues, channels), lambda s: (s, 0, 0))
    return pl.pallas_call(
        body,
        grid=(rows // block,),
        in_specs=[SMEM, *specs],
        out_specs=[
            pl.BlockSpec((block, residues, channels), lambda s: (s, 0, 0)),
            pl.BlockSpec((heads, block, residues), lambda s: (0, s, 0)),
        ],
        out_shape=[
            jax.ShapeDtypeStruct((rows, residues, channels), f32),
            jax.ShapeDtypeStruct((heads, rows, residues), bf16),
        ],
        scratch_shapes=[
            pltpu.VMEM((parts * seqs, (width + 1) * LANES), bf16),
            pltpu.VMEM((parts * seqs, slabs * LANES), bf16),
            pltpu.VMEM((rows, LANES), f32),
            pltpu.VMEM((channels, width * width), bf16),
        ],
        compiler_params=VMEM,
        name="pair_tile",
    )(mine, *operands)


def attend(mine, pieces, gain, kernel, mask, low, high, closing, first, count):
    cols = len(pieces)
    residues, channels = pieces[0].shape[1:]
    arrays = [array for array, offsets in (*low, *high)]
    lists = [offsets for array, offsets in (*low, *high)]
    per_half, side, total = arrays[0].shape[1:]
    heads = 2 * per_half
    inner = closing.shape[0]
    depth = inner // heads
    gain = gain.reshape(1, channels)
    group = LANES // depth
    scale = depth**-0.5 * LOG2E

    def body(mine_ref, gain_ref, kernel_ref, mask_ref, closing_ref, *refs):
        x_refs, refs = refs[:cols], refs[cols:]
        bias_refs, out_refs = refs[: len(arrays)], refs[len(arrays) : -2]
        bias, turned = refs[-2:]

        @pl.when(pl.program_id(0) == 0)
        def _():
            for n, (ref, offsets) in enumerate(zip(bias_refs, lists)):
                start = n // len(low) * per_half
                for e, offset in enumerate(offsets):
                    place = pl.ds(pl.multiple_of((offset ^ mine_ref[2]) * side, 8), side)
                    for h in range(per_half):
                        bias[start + h, place, :] = ref[e, h].astype(f32) * LOG2E
            turned[...] = kernel_ref[:, inner : 2 * inner].T

        row_mask = (mask_ref[0].astype(f32) - 1.0) * (1e9 * LOG2E)
        head_of = lax.broadcasted_iota(jnp.int32, (total, LANES), 1) // depth
        zero = jnp.zeros((depth, total), bf16)
        x = jnp.concatenate([ref[0] for ref in x_refs], 0).astype(f32)
        narrow = (standardize(x) * gain_ref[...]).astype(bf16)
        keys = lax.dot_general(turned[...], narrow, ROWS_BY_ROWS, preferred_element_type=f32).astype(bf16)
        queries, all_values, gates = [
            jnp.dot(narrow, kernel_ref[:, n * inner : (n + 1) * inner], preferred_element_type=f32).astype(bf16)
            for n in (0, 2, 3)
        ]
        spans = [slice(lane, lane + LANES) for lane in range(0, inner, LANES)]
        scores, values = [], []
        for span in spans:
            key, value = keys[span, :], all_values[:, span]
            alone = []
            for h in range(group):
                mine_rows = key[h * depth : (h + 1) * depth]
                alone.append(jnp.concatenate([mine_rows if n == h else zero for n in range(group)], 0))
                here = head_of == h
                values.append(
                    jnp.concatenate(
                        [jnp.where(here, value, jnp.zeros_like(value)), here.astype(f32).astype(bf16)], 1
                    )
                )
            scores.append(jnp.dot(queries[:, span], jnp.concatenate(alone, 1), preferred_element_type=f32))
        weights = []
        for h in range(heads):
            at = h % group * total
            own = scores[h // group][:, at : at + total] * scale + bias[h] + row_mask
            highest = jnp.max(own, axis=1, keepdims=True)
            weights.append(jnp.exp2(own - highest).astype(bf16))
        gated = []
        for n, span in enumerate(spans):
            here = slice(n * group, (n + 1) * group)
            mixed = jnp.dot(
                jnp.concatenate(weights[here], 1), jnp.concatenate(values[here], 0), preferred_element_type=f32
            )
            gate = jax.nn.sigmoid(gates[:, span].astype(f32))
            gated.append((mixed[:, :LANES] / mixed[:, LANES:] * gate).astype(bf16))
        change = jnp.dot(jnp.concatenate(gated, 1), closing_ref[...], preferred_element_type=f32)
        for k in range(cols):
            own = x[k * residues : (k + 1) * residues] + change[k * residues : (k + 1) * residues]
            out_refs[k][0] = own.astype(bf16)

    return pl.pallas_call(
        body,
        grid=(count,),
        in_specs=[
            SMEM,
            whole(gain),
            whole(kernel),
            pl.BlockSpec((1, 1, total), lambda s: (s + first, 0, 0)),
            whole(closing),
        ]
        + [pl.BlockSpec((1, residues, channels), lambda s: (s + first, 0, 0))] * cols
        + [whole(array) for array in arrays],
        out_specs=[pl.BlockSpec((1, residues, channels), lambda s: (s, 0, 0))] * cols,
        out_shape=[jax.ShapeDtypeStruct((count, residues, channels), bf16)] * cols,
        scratch_shapes=[pltpu.VMEM((heads, total, total), f32), pltpu.VMEM((inner, channels), bf16)],
        compiler_params=VMEM,
        name="attend",
    )(mine, gain, kernel, mask, closing, *pieces, *arrays)


def make_shards(mesh):
    n_row, n_col = mesh.shape["row"], mesh.shape["col"]
    halves = n_row // n_col

    def by_row(x, k):
        return lax.ppermute(x, "row", [(r, r ^ k) for r in range(n_row)])

    def by_col(x, k):
        return lax.ppermute(x, "col", [(c, c ^ k) for c in range(n_col)])

    def gather_rows(first, second, others):
        bits = []
        k = 2
        while k < n_row:
            bits.append(k)
            k *= 2
        held = [(first[None], [0]), (second[None], [0])]
        for step in range(len(bits)):
            got = []
            for part, k in ((0, bits[step]), (1, bits[-1 - step])):
                array, offsets = held[part]
                got.append(
                    (jnp.concatenate([array, by_row(array, k)], 0), offsets + [o ^ k for o in offsets])
                )
            held = got
        arrays, others = lax.optimization_barrier(([array for array, offsets in held], others))
        sides = [
            [(array, offsets), (by_row(array, 1), [o ^ 1 for o in offsets])]
            for array, (_, offsets) in zip(arrays, held)
        ]
        return (*sides, others)

    def shards(
        msa,
        available,
        chain_site_available,
        duo_embedding,
        averaging_gain,
        lineup_gain,
        duo_gain,
        left_kernel,
        right_kernel,
        kronecker_kernel,
        logit_kernel,
        projection_kernel,
        closing_kernel,
    ):
        seqs, residues, channels = msa.shape
        rows = duo_embedding.shape[0]
        r, c = lax.axis_index("row"), lax.axis_index("col")
        share = seqs // n_col
        mine = jnp.stack([r, c, r ^ (halves * c)]).astype(jnp.int32)

        left, right = opm_inputs(msa, available, averaging_gain, left_kernel, right_kernel, rows)
        rights = lax.all_gather(right, "row", axis=0)
        spread = lax.all_gather(left, "col", axis=0, tiled=True)
        left_rows = lax.all_to_all(spread, "row", 0, 0, tiled=True)

        x = [lax.dynamic_slice_in_dim(msa, (c ^ k) * share, share, 0) for k in range(n_col)]
        x, spread_late = lax.optimization_barrier((x, spread))
        soon = max(n_col - 1, 2)
        x = [by_col(piece, k) if 0 < k < soon else piece for k, piece in enumerate(x)]
        mask = lax.dynamic_slice_in_dim(spread_late[:, -1, :, :rows], c * share, share, 1)
        mask = mask.reshape(n_col, halves, share, rows)
        mask = jnp.stack([lax.dynamic_index_in_dim(mask, c ^ k, 0, keepdims=False) for k in range(n_col)])
        rows_mask = mask.transpose(2, 0, 1, 3).reshape(share, 1, residues * n_col)

        left_rows, rows_mask = lax.optimization_barrier((left_rows, rows_mask))
        duo_after_averaging, tile = pair_tile(
            mine,
            left_rows,
            rights,
            duo_embedding,
            chain_site_available.reshape(1, -1),
            kronecker_kernel,
            duo_gain,
            logit_kernel,
        )
        tile, x[1:soon] = lax.optimization_barrier((tile, x[1:soon]))
        tiles = [tile] + [by_col(tile, k) for k in range(1, n_col)]
        cut = tile.shape[0] // 2
        tiles, x[soon:] = lax.optimization_barrier((tiles, x[soon:]))
        x[soon:] = [by_col(piece, k) for k, piece in enumerate(x[soon:], soon)]
        low, high, x[soon:] = gather_rows(
            jnp.concatenate([t[:cut] for t in tiles], 2), jnp.concatenate([t[cut:] for t in tiles], 2), x[soon:]
        )
        sent = []
        first = 0
        for count in chunks(share):
            held = rows_mask
            if len(sent) > 1:
                held, sent[-2] = lax.optimization_barrier((rows_mask, sent[-2]))
            outs = attend(
                mine, x, lineup_gain, projection_kernel, held, low, high, closing_kernel, first, count
            )
            sent.append([by_col(piece, k) if k else piece for k, piece in enumerate(outs)])
            first += count
        refreshed = jnp.zeros_like(msa)
        first = 0
        for count, parts in zip(chunks(share), sent):
            for k, piece in enumerate(parts):
                refreshed = lax.dynamic_update_slice_in_dim(refreshed, piece, (c ^ k) * share + first, 0)
            first += count
        return refreshed, duo_after_averaging

    return shards


def chunks(share):
    most = max(-(-3 * share // 8), 1)
    counts = []
    while sum(counts) < share:
        counts.append(min(most, share - sum(counts)))
    return counts


def solution(mesh):
    split = P("row", "col", None)
    placed = (split, P("row", "col"), P(), split, P(), P(), P(), P(), P(), P(), P(), P(), P())
    return jax.shard_map(
        make_shards(mesh), mesh=mesh, in_specs=placed, out_specs=(split, split), check_vma=False
    )
```

```python
import math

import jax
import jax.numpy as jnp
from jax import lax
from jax.experimental import pallas as pl
from jax.experimental.pallas import tpu as pltpu
from jax.sharding import PartitionSpec as P

EPSILON = 1e-05
LOG2E = math.log2(math.e)
LANES = 128
ROWS_BY_ROWS = (((1,), (1,)), ((), ()))
CONTRACT_FIRST = (((0,), (0,)), ((), ()))
VMEM = pltpu.CompilerParams(vmem_limit_bytes=56 * 2**20)
SMEM = pl.BlockSpec(memory_space=pltpu.SMEM)
f32 = jnp.float32
bf16 = jnp.bfloat16


def whole(array):
    return pl.BlockSpec(array.shape, lambda step, rank=array.ndim: (0,) * rank)


def standardize(values):
    average = jnp.mean(values, axis=-1, keepdims=True)
    centred = values - average
    variance = jnp.mean(centred * centred, axis=-1, keepdims=True)
    return centred * lax.rsqrt(variance + EPSILON)


def opm_inputs_kernel(x_ref, mask_ref, gain_ref, wl_ref, wr_ref, left_ref, right_ref, scratch):
    seqs, residues, channels = x_ref.shape
    width = wr_ref.shape[0]
    per_group = LANES // width
    left_weight = wl_ref[...].astype(f32).T
    groups = residues // per_group
    halves, slabs = left_ref.shape[:2]
    half_groups = slabs - 1
    half_residues = residues // halves
    normed = standardize(x_ref[...].reshape(seqs * residues, channels).astype(f32)) * gain_ref[...]
    for piece in range(channels // LANES):
        scratch[piece] = normed[:, piece * LANES : (piece + 1) * LANES]
    narrow = normed.astype(bf16).reshape(seqs, residues, channels)
    mask = mask_ref[...].astype(f32)
    right = [
        lax.dot_general(wr_ref[...], narrow[s], ROWS_BY_ROWS, preferred_element_type=f32) * mask[s : s + 1, :]
        for s in range(seqs)
    ]
    right_ref[:width] = jnp.swapaxes(jnp.stack(right, 0), 0, 1).astype(bf16)
    right_ref[width] = mask.astype(bf16)
    total = None
    for q in range(per_group):
        rows = jnp.concatenate(
            [scratch[piece, pl.ds(q, seqs * groups, stride=per_group), :] for piece in range(channels // LANES)], 1
        ).astype(bf16)
        sides = [jnp.zeros((channels, q * width), f32), jnp.zeros((channels, LANES - (q + 1) * width), f32)]
        placed = jnp.concatenate([a for a in (sides[0], left_weight, sides[1]) if a.shape[1]], 1).astype(bf16)
        part = jnp.dot(rows, placed, preferred_element_type=f32)
        total = part if total is None else total + part
    left = jnp.swapaxes(total.reshape(seqs, groups, LANES), 0, 1)
    row = lax.broadcasted_iota(jnp.int32, (residues, residues * width), 0) * width
    col = lax.broadcasted_iota(jnp.int32, (residues, residues * width), 1)
    spread = ((col >= row) & (col < row + width)).astype(f32).astype(bf16)
    mask_wide = jnp.dot(mask.astype(bf16), spread, preferred_element_type=f32)
    for g in range(groups):
        left_ref[g // half_groups, g % half_groups] = (left[g] * mask_wide[:, g * LANES : (g + 1) * LANES]).astype(bf16)
    for half in range(halves):
        part = mask[:, half * half_residues : (half + 1) * half_residues]
        left_ref[half, half_groups] = jnp.concatenate(
            [part, jnp.zeros((seqs, LANES - half_residues), f32)], 1
        ).astype(bf16)


def opm_inputs(x, mask, gain, wl, wr, half_residues, block=16):
    seqs, residues, channels = x.shape
    width = wl.shape[1]
    per_group = LANES // width
    halves = residues // half_residues
    slabs = half_residues // per_group + 1
    gain = gain.reshape(1, channels)
    return pl.pallas_call(
        opm_inputs_kernel,
        grid=(seqs // block,),
        in_specs=[
            pl.BlockSpec((block, residues, channels), lambda s: (s, 0, 0)),
            pl.BlockSpec((block, residues), lambda s: (s, 0)),
            whole(gain),
            whole(wl.T),
            whole(wr.T),
        ],
        out_specs=[
            pl.BlockSpec((halves, slabs, block, LANES), lambda s: (0, 0, s, 0)),
            pl.BlockSpec((width + 1, block, residues), lambda s: (0, s, 0)),
        ],
        out_shape=[
            jax.ShapeDtypeStruct((halves, slabs, seqs, LANES), bf16),
            jax.ShapeDtypeStruct((width + 1, seqs, residues), bf16),
        ],
        scratch_shapes=[pltpu.VMEM((channels // LANES, block * residues, LANES), f32)],
        compiler_params=VMEM,
        name="opm_inputs",
    )(x, mask, gain, wl.T, wr.T)


def pair_tile(mine, left, right, duo, chain, kernel, gain, logit, block=16):
    rows, residues, channels = duo.shape
    heads = logit.shape[1]
    parts, slabs, seqs = left.shape[:3]
    groups = slabs - 1
    width = right.shape[1] - 1

    def body(mine_ref, left_ref, right_ref, *refs):
        duo_ref, chain_ref, kernel_ref, gain_ref, logit_ref, out_ref, bias_ref, rhs, lhs, scale, w_ref = refs
        step = pl.program_id(0)

        @pl.when(step == 0)
        def _():
            for n in range(parts):
                for b in range(width + 1):
                    rhs[n * seqs : (n + 1) * seqs, b * LANES : b * LANES + residues] = right_ref[n, b]
                for g in range(slabs):
                    lhs[n * seqs : (n + 1) * seqs, g * LANES : (g + 1) * LANES] = left_ref[n, g]
            counts = lax.dot_general(
                lhs[:, groups * LANES :], rhs[:, width * LANES :], CONTRACT_FIRST, preferred_element_type=f32
            )[:rows, :residues]
            flags = chain_ref[...].astype(f32)
            both_flags = []
            for size, at in ((rows, mine_ref[0] * rows), (residues, mine_ref[1] * residues)):
                place = lax.broadcasted_iota(jnp.int32, (chain.shape[1], size), 0)
                pick = place == lax.broadcasted_iota(jnp.int32, (chain.shape[1], size), 1) + at
                both_flags.append(jnp.dot(flags, pick.astype(f32), preferred_element_type=f32))
            present = lax.dot_general(*both_flags, CONTRACT_FIRST, preferred_element_type=f32)
            scale[:, :residues] = present / (counts + 0.001)
            mixing = jnp.swapaxes(kernel_ref[...].astype(f32).reshape(width, width, channels), 0, 1)
            w_ref[...] = mixing.reshape(width * width, channels).T.astype(bf16)

        span = block * width
        picked = lhs[:, pl.ds(pl.multiple_of(step * span, LANES), span)]
        outer = lax.dot_general(
            picked, rhs[:, : width * LANES], CONTRACT_FIRST, preferred_element_type=f32
        ).astype(bf16)
        row_scale = scale[pl.ds(pl.multiple_of(step * block, 8), block), :]
        biases = []
        every = [
            jnp.concatenate(
                [outer[i * width : (i + 1) * width, b * LANES : (b + 1) * LANES] for b in range(width)], 0
            )
            for i in range(block)
        ]
        update = jnp.dot(w_ref[...], jnp.concatenate(every, 1), preferred_element_type=f32)
        fresh = []
        for i in range(block):
            mine = (update[:, i * LANES : (i + 1) * LANES] * row_scale[i : i + 1, :]).T[:residues]
            fresh.append(duo_ref[i] + mine)
            out_ref[i] = fresh[-1]
        pair_input = (standardize(jnp.concatenate(fresh, 0)) * gain_ref[...]).astype(bf16)
        for i in range(block):
            own = pair_input[i * residues : (i + 1) * residues]
            biases.append(lax.dot_general(logit_ref[...], own, ROWS_BY_ROWS, preferred_element_type=f32))
        bias_ref[...] = jnp.swapaxes(jnp.stack(biases, 0), 0, 1).astype(bf16)

    operands = [
        left,
        right,
        duo,
        chain,
        kernel,
        gain.reshape(1, channels),
        logit.T,
    ]
    specs = [whole(array) for array in operands]
    specs[2] = pl.BlockSpec((block, residues, channels), lambda s: (s, 0, 0))
    return pl.pallas_call(
        body,
        grid=(rows // block,),
        in_specs=[SMEM, *specs],
        out_specs=[
            pl.BlockSpec((block, residues, channels), lambda s: (s, 0, 0)),
            pl.BlockSpec((heads, block, residues), lambda s: (0, s, 0)),
        ],
        out_shape=[
            jax.ShapeDtypeStruct((rows, residues, channels), f32),
            jax.ShapeDtypeStruct((heads, rows, residues), bf16),
        ],
        scratch_shapes=[
            pltpu.VMEM((parts * seqs, (width + 1) * LANES), bf16),
            pltpu.VMEM((parts * seqs, slabs * LANES), bf16),
            pltpu.VMEM((rows, LANES), f32),
            pltpu.VMEM((channels, width * width), bf16),
        ],
        compiler_params=VMEM,
        name="pair_tile",
    )(mine, *operands)


def attend(mine, pieces, starts, gain, kernel, mask, low, high, closing, first, count):
    cols = len(pieces)
    residues, channels = pieces[0].shape[1:]
    arrays = [array for array, offsets in (*low, *high)]
    lists = [offsets for array, offsets in (*low, *high)]
    per_half, side, total = arrays[0].shape[1:]
    heads = 2 * per_half
    inner = closing.shape[0]
    depth = inner // heads
    gain = gain.reshape(1, channels)
    group = LANES // depth
    scale = depth**-0.5 * LOG2E

    def body(mine_ref, gain_ref, kernel_ref, mask_ref, closing_ref, *refs):
        x_refs, refs = refs[:cols], refs[cols:]
        bias_refs, out_refs = refs[: len(arrays)], refs[len(arrays) : -2]
        bias, turned = refs[-2:]

        @pl.when(pl.program_id(0) == 0)
        def _():
            for n, (ref, offsets) in enumerate(zip(bias_refs, lists)):
                start = n // len(low) * per_half
                for e, offset in enumerate(offsets):
                    place = pl.ds(pl.multiple_of((offset ^ mine_ref[2]) * side, 8), side)
                    for h in range(per_half):
                        bias[start + h, place, :] = ref[e, h].astype(f32) * LOG2E
            turned[...] = kernel_ref[:, inner : 2 * inner].T

        row_mask = (mask_ref[0].astype(f32) - 1.0) * (1e9 * LOG2E)
        head_of = lax.broadcasted_iota(jnp.int32, (total, LANES), 1) // depth
        zero = jnp.zeros((depth, total), bf16)
        x = jnp.concatenate([ref[0] for ref in x_refs], 0).astype(f32)
        narrow = (standardize(x) * gain_ref[...]).astype(bf16)
        keys = lax.dot_general(turned[...], narrow, ROWS_BY_ROWS, preferred_element_type=f32).astype(bf16)
        queries, all_values, gates = [
            jnp.dot(narrow, kernel_ref[:, n * inner : (n + 1) * inner], preferred_element_type=f32).astype(bf16)
            for n in (0, 2, 3)
        ]
        spans = [slice(lane, lane + LANES) for lane in range(0, inner, LANES)]
        scores, values = [], []
        for span in spans:
            key, value = keys[span, :], all_values[:, span]
            alone = []
            for h in range(group):
                mine_rows = key[h * depth : (h + 1) * depth]
                alone.append(jnp.concatenate([mine_rows if n == h else zero for n in range(group)], 0))
                here = head_of == h
                values.append(
                    jnp.concatenate(
                        [jnp.where(here, value, jnp.zeros_like(value)), here.astype(f32).astype(bf16)], 1
                    )
                )
            scores.append(jnp.dot(queries[:, span], jnp.concatenate(alone, 1), preferred_element_type=f32))
        weights = []
        for h in range(heads):
            at = h % group * total
            own = scores[h // group][:, at : at + total] * scale + bias[h] + row_mask
            highest = jnp.max(own, axis=1, keepdims=True)
            weights.append(jnp.exp2(own - highest).astype(bf16))
        gated = []
        for n, span in enumerate(spans):
            here = slice(n * group, (n + 1) * group)
            mixed = jnp.dot(
                jnp.concatenate(weights[here], 1), jnp.concatenate(values[here], 0), preferred_element_type=f32
            )
            gate = jax.nn.sigmoid(gates[:, span].astype(f32))
            gated.append((mixed[:, :LANES] / mixed[:, LANES:] * gate).astype(bf16))
        change = jnp.dot(jnp.concatenate(gated, 1), closing_ref[...], preferred_element_type=f32)
        for k in range(cols):
            own = x[k * residues : (k + 1) * residues] + change[k * residues : (k + 1) * residues]
            out_refs[k][0] = own.astype(bf16)

    return pl.pallas_call(
        body,
        grid=(count,),
        in_specs=[
            SMEM,
            whole(gain),
            whole(kernel),
            pl.BlockSpec((1, 1, total), lambda s: (s + first, 0, 0)),
            whole(closing),
        ]
        + [pl.BlockSpec((1, residues, channels), lambda s, at=at: (s + at, 0, 0)) for at in starts]
        + [whole(array) for array in arrays],
        out_specs=[pl.BlockSpec((1, residues, channels), lambda s: (s, 0, 0))] * cols,
        out_shape=[jax.ShapeDtypeStruct((count, residues, channels), bf16)] * cols,
        scratch_shapes=[pltpu.VMEM((heads, total, total), f32), pltpu.VMEM((inner, channels), bf16)],
        compiler_params=VMEM,
        name="attend",
    )(mine, gain, kernel, mask, closing, *pieces, *arrays)


def make_shards(mesh):
    n_row, n_col = mesh.shape["row"], mesh.shape["col"]
    halves = n_row // n_col

    def by_row(x, k):
        return lax.ppermute(x, "row", [(r, r ^ k) for r in range(n_row)])

    def by_col(x, k):
        return lax.ppermute(x, "col", [(c, c ^ k) for c in range(n_col)])

    def gather_rows(first, second, others):
        bits = []
        k = 2
        while k < n_row:
            bits.append(k)
            k *= 2
        held = [(first[None], [0]), (second[None], [0])]
        for step in range(len(bits)):
            got = []
            for part, k in ((0, bits[step]), (1, bits[-1 - step])):
                array, offsets = held[part]
                got.append(
                    (jnp.concatenate([array, by_row(array, k)], 0), offsets + [o ^ k for o in offsets])
                )
            held = got
        arrays, others = lax.optimization_barrier(([array for array, offsets in held], others))
        sides = [
            [(array, offsets), (by_row(array, 1), [o ^ 1 for o in offsets])]
            for array, (_, offsets) in zip(arrays, held)
        ]
        return (*sides, others)

    def shards(
        msa,
        available,
        chain_site_available,
        duo_embedding,
        averaging_gain,
        lineup_gain,
        duo_gain,
        left_kernel,
        right_kernel,
        kronecker_kernel,
        logit_kernel,
        projection_kernel,
        closing_kernel,
    ):
        seqs, residues, channels = msa.shape
        rows = duo_embedding.shape[0]
        r, c = lax.axis_index("row"), lax.axis_index("col")
        share = seqs // n_col
        mine = jnp.stack([r, c, r ^ (halves * c)]).astype(jnp.int32)

        left, right = opm_inputs(msa, available, averaging_gain, left_kernel, right_kernel, rows)
        rights = lax.all_gather(right, "row", axis=0)
        spread = lax.all_gather(left, "col", axis=0, tiled=True)
        left_rows = lax.all_to_all(spread, "row", 0, 0, tiled=True)

        x = [lax.dynamic_slice_in_dim(msa, (c ^ k) * share, share, 0) for k in range(n_col)]
        x, spread_late = lax.optimization_barrier((x, spread))
        soon = max(n_col - 1, 2)
        x = [by_col(piece, k) if 0 < k < soon else piece for k, piece in enumerate(x)]
        mask = lax.dynamic_slice_in_dim(spread_late[:, -1, :, :rows], c * share, share, 1)
        mask = mask.reshape(n_col, halves, share, rows)
        mask = jnp.stack([lax.dynamic_index_in_dim(mask, c ^ k, 0, keepdims=False) for k in range(n_col)])
        rows_mask = mask.transpose(2, 0, 1, 3).reshape(share, 1, residues * n_col)

        left_rows, rows_mask = lax.optimization_barrier((left_rows, rows_mask))
        duo_after_averaging, tile = pair_tile(
            mine,
            left_rows,
            rights,
            duo_embedding,
            chain_site_available.reshape(1, -1),
            kronecker_kernel,
            duo_gain,
            logit_kernel,
        )
        tile, x[1:soon] = lax.optimization_barrier((tile, x[1:soon]))
        tiles = [tile] + [by_col(tile, k) for k in range(1, n_col)]
        cut = tile.shape[0] // 2
        tiles, x[soon:] = lax.optimization_barrier((tiles, x[soon:]))
        lead = chunks(share)[0]
        rest = [by_col(piece[lead:], k) for k, piece in enumerate(x[soon:], soon)] if lead < share else []
        x[soon:] = [by_col(piece[:lead], k) for k, piece in enumerate(x[soon:], soon)]
        low, high, x[soon:] = gather_rows(
            jnp.concatenate([t[:cut] for t in tiles], 2), jnp.concatenate([t[cut:] for t in tiles], 2), x[soon:]
        )
        sent = []
        first = 0
        for count in chunks(share):
            held = rows_mask
            now = [*x[:soon], *(x[soon:] if not first else rest)]
            starts = [first] * soon + [max(first - lead, 0)] * (n_col - soon)
            if len(sent) > 1:
                held, sent[-2] = lax.optimization_barrier((rows_mask, sent[-2]))
            outs = attend(
                mine, now, starts, lineup_gain, projection_kernel, held, low, high, closing_kernel, first, count
            )
            sent.append([by_col(piece, k) if k else piece for k, piece in enumerate(outs)])
            first += count
        refreshed = jnp.zeros_like(msa)
        first = 0
        for count, parts in zip(chunks(share), sent):
            for k, piece in enumerate(parts):
                refreshed = lax.dynamic_update_slice_in_dim(refreshed, piece, (c ^ k) * share + first, 0)
            first += count
        return refreshed, duo_after_averaging

    return shards


def chunks(share):
    most = max(-(-3 * share // 8), 1)
    counts = []
    while sum(counts) < share:
        counts.append(min(most, share - sum(counts)))
    return counts


def solution(mesh):
    split = P("row", "col", None)
    placed = (split, P("row", "col"), P(), split, P(), P(), P(), P(), P(), P(), P(), P(), P())
    return jax.shard_map(
        make_shards(mesh), mesh=mesh, in_specs=placed, out_specs=(split, split), check_vma=False
    )
```
